32 devices in a mesh: expert: 16 (over z, y, x), tensor: 2 (over core).
Axes of the slice: x: 2, y: 2, z: 4, core: 2. Of those that a mesh axis runs over, the one named last changes fastest.
Arguments:
- cotangent: bfloat16 [2048, 4096], P('expert', 'tensor'), may hold values from -1.5 to 1.5
- routes: int32 [2048, 2], P('expert'), may hold values from 0 to 15, all different within a row; in each aligned block of 128 rows (0 to 127, 128 to 255, ...) at most 32 rows name the same one
- router_weight: float32 [2048, 2], P('expert'), may hold values from 0.1 to 0.9
- clients: int32 [2048], P('expert'), may hold values from 0 to 3
- gate_preactivation: bfloat16 [16, 512, 3072], P('expert', None, 'tensor'), may hold values from -6 to 6
- up_preactivation: bfloat16 [16, 512, 3072], P('expert', None, 'tensor'), may hold values from -6 to 6
- down_matrix: bfloat16 [16, 3072, 4096], P('expert', 'tensor'), may hold values from -0.109375 to 0.109375
- adapter_input_maps: bfloat16 [16, 3072, 64], P('expert', 'tensor'), may hold values from -0.359375 to 0.359375
- adapter_output_maps: bfloat16 [16, 64, 4096], P('expert', None, 'tensor'), may hold values from -0.09375 to 0.09375
Outputs:
- gate_grad: float32 [2048, 2], P('expert')
- grad_gate_pre: bfloat16 [16, 512, 3072], P('expert', None, 'tensor')
- grad_up_pre: bfloat16 [16, 512, 3072], P('expert', None, 'tensor')
- grad_lora_a: float32 [16, 3072, 64], P('expert', 'tensor')
- grad_lora_b: float32 [16, 64, 4096], P('expert', None, 'tensor')
The draws below stay inside these ranges and needn't reach their ends.
Inputs may be any that keep to these rules, and one draw needn't show every extreme that they name: `routes`: the 2 experts of a token differ. Among the 128 tokens of one device no expert is named more than 32 times, and in every draw some expert is named exactly 32 times by the tokens of some device.
All inputs are finite; a program needn't handle non-finite values.
Results may differ from the reference program's by a relative error of at most 0.0049.
Values may be sent and summed in bfloat16 or wider, within the bound.
A program may use at most 64 MiB of HBM per device.

```python
import math
import jax
import jax.numpy as jnp
import numpy as np
from jax import lax

MODEL_WIDTH = 4096
HIDDEN_UNITS = 3072
ADAPTER_RANK = 16
CLIENT_COUNT = 4
TOP = 2
TOK_DEV = 128
TOKENS = 2048
EXPERT_COUNT = 16
SEND = 32
CAP = 512
N_EXPERT = 16


def plant(result, stream_key, smallest, largest):
    dims = result.shape
    index_at = [jax.random.randint(jax.random.fold_in(stream_key, axis), (), 0, dims[axis]) for axis in range(len(dims))]
    result = result.at[tuple(index_at)].set(smallest)
    longest = dims.index(max(dims))
    index_at[longest] = (index_at[longest] + 1) % dims[longest]
    return result.at[tuple(index_at)].set(largest)


def shard_levels(stream_key, dims, split, smallest, largest):
    def one(position, shards_of):
        heights = jax.random.uniform(jax.random.fold_in(jax.random.fold_in(stream_key, 6), position), (shards_of,), jnp.float32, smallest / len(split), largest / len(split))
        return jnp.repeat(jnp.exp(heights), dims[position] // shards_of).reshape((-1,) + (1,) * (len(dims) - position - 1))

    loudness = one(*split[0])
    for cut in split[1:]:
        loudness = loudness * one(*cut)
    return loudness


def assign_block(key, own, number, rows, number_of, top, reach, skew):
    sequence = jax.random.permutation(key, number_of)
    packed, usual = shares(number_of, rows * top, reach, skew, True), shares(number_of, rows * top, reach, skew, False)
    places = jnp.arange(number_of)

    def named(lengths, offset_by):
        used = int((lengths > 0).sum())
        fixed = max(1, used // 4)
        shifted = fixed + (places - fixed + offset_by * (used - fixed)) % max(1, number_of - fixed)
        return jnp.zeros((number_of,), jnp.int32).at[sequence[jnp.where(places < fixed, places, shifted)]].set(jnp.asarray(lengths, jnp.int32))

    lengths = jnp.where(number % 4 == 0, named(packed, number // 4), named(usual, number - number // 4 - 1))
    mixed = jax.random.permutation(jax.random.fold_in(own, 3), number_of)
    source_of, receiver = mixed[0:number_of // 2 * 2:2], mixed[1:number_of // 2 * 2:2]
    margin = jnp.minimum(lengths[source_of] - 1, reach - lengths[receiver]) // 2
    margin = jnp.where((source_of == sequence[0]) | (receiver == sequence[0]) | (lengths[receiver] == 0), 0, jnp.maximum(margin, 0))
    shifted = jax.random.randint(jax.random.fold_in(own, 4), (number_of // 2,), 0, 1 << 20) % (margin + 1)
    lengths = lengths.at[source_of].add(-shifted).at[receiver].add(shifted)
    items = jnp.searchsorted(jnp.cumsum(lengths), jnp.arange(rows * top), side="right").astype(jnp.int32)
    listing = items.reshape(top, rows).T
    listing = listing[jax.random.permutation(jax.random.fold_in(own, 1), rows)]
    offset_by = jax.random.randint(jax.random.fold_in(own, 2), (rows, 1), 0, top)
    return jnp.take_along_axis(listing, (jnp.arange(top)[None, :] + offset_by) % top, axis=1)


def shares(number_of, total, most, skew, full):
    portions = [(1 << 20) // math.isqrt(standing ** skew) + 1 for standing in range(1, number_of + 1)]
    largest = most if full else min(most, max(-(-total // number_of), total * portions[0] // sum(portions)))
    least = 1 if total - largest >= number_of - 1 else 0
    counts, surplus = [largest] + [least] * (number_of - 1), total - largest - least * (number_of - 1)
    while surplus > 0:
        movable = [i for i in range(1, number_of) if counts[i] < largest] or [i for i in range(1, number_of) if counts[i] < most]
        mass, budget = sum([portions[i] for i in movable]), surplus
        for i in movable:
            more = min(most - counts[i], max(1, budget * portions[i] // mass), surplus)
            counts[i] = counts[i] + more
            surplus = surplus - more
    return np.array(counts)


def normal_values(key, shape, spread, reach, split=(), kind=jnp.bfloat16):
    entries = jax.random.normal(key, shape, jnp.float32) * spread
    if len(split) > 0:
        entries = shard_levels(key, shape, split, -0.22, 0.18) * entries
    return jnp.clip(entries, min=-reach, max=reach).astype(kind)


def setup_inputs(seed: int = 0) -> dict:
    seeds = jax.random.split(jax.random.key(seed), 10)
    cotangent = normal_values(seeds[0], (TOKENS, MODEL_WIDTH), 0.25, 1.5, ((0, 16), (1, 2)))
    routes_keys = jax.random.split(jax.random.fold_in(seeds[1], 1), TOKENS // TOK_DEV)
    routes_turns = jax.random.permutation(jax.random.fold_in(seeds[1], 3), TOKENS // TOK_DEV)
    routes = jax.vmap(lambda own, number: assign_block(jax.random.fold_in(seeds[1], 2), own, number, TOK_DEV, EXPERT_COUNT, TOP, SEND, 2))(routes_keys, routes_turns).reshape((TOKENS, TOP))
    router_weight = jnp.clip(0.1 + 0.79999997 * jax.random.uniform(seeds[2], (TOKENS, TOP), jnp.float32) ** shard_levels(seeds[2], (TOKENS, TOP), ((0, 16),), -0.2, 0.2), 0.1, 0.9)
    clients = plant(jax.random.randint(seeds[3], (TOKENS,), 0, CLIENT_COUNT), jax.random.fold_in(seeds[3], 1), 0, CLIENT_COUNT - 1).astype(jnp.int32)
    gate_preactivation = normal_values(seeds[4], (EXPERT_COUNT, CAP, HIDDEN_UNITS), 1.0, 6.0, ((0, 16), (2, 2)))
    up_preactivation = normal_values(seeds[5], (EXPERT_COUNT, CAP, HIDDEN_UNITS), 1.0, 6.0, ((0, 16), (2, 2)))
    down_matrix = normal_values(seeds[6], (EXPERT_COUNT, HIDDEN_UNITS, MODEL_WIDTH), HIDDEN_UNITS ** -0.5, 0.109375, ((0, 16), (1, 2)))
    adapter_input_maps = normal_values(seeds[7], (EXPERT_COUNT, HIDDEN_UNITS, CLIENT_COUNT * ADAPTER_RANK), 0.06, 0.359375, ((0, 16), (1, 2)))
    adapter_output_maps = normal_values(seeds[8], (EXPERT_COUNT, CLIENT_COUNT * ADAPTER_RANK, MODEL_WIDTH), MODEL_WIDTH ** -0.5, 0.09375, ((0, 16), (2, 2)))
    return dict(cotangent=cotangent, routes=routes, router_weight=router_weight, clients=clients, gate_preactivation=gate_preactivation, up_preactivation=up_preactivation, down_matrix=down_matrix, adapter_input_maps=adapter_input_maps, adapter_output_maps=adapter_output_maps)


adapter_scale = 2.0


def silu_parts(gate):
    sig = jax.nn.sigmoid(gate)
    return gate * sig, sig * (1.0 + gate * (1.0 - sig))


def expert_wise(items):
    expert_rows, pick_weight, picked_slots, gate_e, up_e, down_e, a_e, b_e = items
    client_mask = jnp.repeat(picked_slots, ADAPTER_RANK, axis=1)
    act, slope = silu_parts(gate_e.astype(jnp.float32))
    up_full = up_e.astype(jnp.float32)
    hidden_units = act * up_full
    hidden_lowrank = hidden_units.astype(jnp.bfloat16)
    contract_dims = (((1,), (1,)), ((), ()))
    frozen_output = lax.dot_general(expert_rows, down_e, contract_dims, preferred_element_type=jnp.float32)
    adapter_output = lax.dot_general(expert_rows, b_e, contract_dims, preferred_element_type=jnp.float32) * client_mask
    projected_rows = jnp.dot(hidden_lowrank, a_e, preferred_element_type=jnp.float32) * client_mask
    backward_result = lax.dot_general(adapter_output.astype(jnp.bfloat16), a_e, contract_dims, preferred_element_type=jnp.float32)
    hidden_gradient = pick_weight[:, None] * (frozen_output + adapter_scale * backward_result)
    gate_gradient = (hidden_gradient * up_full * slope).astype(jnp.bfloat16)
    up_gradient = (hidden_gradient * act).astype(jnp.bfloat16)
    row_dimensions = (((0,), (0,)), ((), ()))
    input_map_gradient = adapter_scale * lax.dot_general(hidden_lowrank, (pick_weight[:, None] * adapter_output).astype(jnp.bfloat16), row_dimensions, preferred_element_type=jnp.float32)
    output_map_gradient = adapter_scale * lax.dot_general((pick_weight[:, None] * projected_rows).astype(jnp.bfloat16), expert_rows, row_dimensions, preferred_element_type=jnp.float32)
    slot_gradient = jnp.sum(hidden_units * frozen_output, axis=1) + adapter_scale * jnp.sum(projected_rows * adapter_output, axis=1)
    return gate_gradient, up_gradient, input_map_gradient, output_map_gradient, slot_gradient


def reference(cotangent, routes, router_weight, clients, gate_preactivation, up_preactivation, down_matrix, adapter_input_maps, adapter_output_maps):
    picks = routes.reshape(N_EXPERT, TOK_DEV * TOP)
    onehot = (picks[:, :, None] == jnp.arange(EXPERT_COUNT, dtype=jnp.int32)).astype(jnp.int32)
    before = jnp.cumsum(onehot, axis=1) - onehot
    rank = jnp.sum(before * onehot, axis=2)
    source = jnp.arange(N_EXPERT, dtype=jnp.int32)[:, None]
    slot = (picks * CAP + source * SEND + rank).reshape(-1).astype(jnp.int32)
    owner = (jnp.arange(TOKENS * TOP, dtype=jnp.int32) // TOP).astype(jnp.int32)
    token_rows = jnp.zeros((EXPERT_COUNT * CAP, MODEL_WIDTH), cotangent.dtype).at[slot].set(cotangent[owner]).reshape(EXPERT_COUNT, CAP, MODEL_WIDTH)
    pick_weight = jnp.zeros((EXPERT_COUNT * CAP,), jnp.float32).at[slot].set(router_weight.reshape(-1).astype(jnp.float32)).reshape(EXPERT_COUNT, CAP)
    client_hot = (clients[owner][:, None] == jnp.arange(CLIENT_COUNT, dtype=jnp.int32)).astype(jnp.float32)
    picked_slots = jnp.zeros((EXPERT_COUNT * CAP, CLIENT_COUNT), jnp.float32).at[slot].set(client_hot).reshape(EXPERT_COUNT, CAP, CLIENT_COUNT)
    gate_gradient, up_gradient, input_map_gradient, output_map_gradient, slot_gradient = lax.map(expert_wise, (token_rows, pick_weight, picked_slots, gate_preactivation, up_preactivation, down_matrix, adapter_input_maps, adapter_output_maps))
    gate_grad = slot_gradient.reshape(-1)[slot].reshape(TOKENS, TOP)
    return gate_grad, gate_gradient, up_gradient, input_map_gradient, output_map_gradient
```

```python
import functools

import jax
import jax.numpy as jnp
from jax import lax
from jax.sharding import PartitionSpec as P

ADAPTER_RANK = 16


adapter_scale = 2.0


def silu_parts(gate):
    sig = jax.nn.sigmoid(gate)
    return (gate * sig, sig * (1.0 + gate * (1.0 - sig)))


def local(
    cotangent,
    routes,
    router_weight,
    clients,
    gate_preactivation,
    up_preactivation,
    down_matrix,
    adapter_input_maps,
    adapter_output_maps,
):
    experts = lax.axis_size("expert")
    tok_rows = cotangent.shape[0]
    width = cotangent.shape[1]
    picks_per = routes.shape[1]
    slots = gate_preactivation.shape[1]
    per_source = slots // experts
    adapter_groups = adapter_input_maps.shape[2] // ADAPTER_RANK
    token_ids = jnp.arange(tok_rows, dtype=jnp.int32)
    expert_ids = jnp.arange(experts, dtype=jnp.int32)
    slot_ids = jnp.arange(experts * per_source, dtype=jnp.int32)
    hits = (routes[:, :, None] == expert_ids).astype(jnp.float32)
    earlier = (token_ids[:, None] > token_ids[None, :]).astype(jnp.bfloat16)
    before = jnp.dot(
        earlier, jnp.sum(hits, axis=1).astype(jnp.bfloat16), preferred_element_type=jnp.float32
    )
    rank = jnp.sum(before[:, None, :] * hits, axis=2).astype(jnp.int32)
    slot = routes * per_source + rank
    chosen = [slot_ids[:, None] == slot[None, :, k] for k in range(picks_per)]
    filled = functools.reduce(jnp.logical_or, chosen)
    weight_slots = sum(
        jnp.sum(jnp.where(chosen[k], router_weight[None, :, k], 0.0), axis=1)
        for k in range(picks_per)
    )
    client_slots = jnp.sum(
        jnp.where(filled, (clients[None, :] + 1).astype(jnp.float32), 0.0), axis=1
    )
    facts = jnp.concatenate(
        [weight_slots.reshape(experts, per_source), client_slots.reshape(experts, per_source)],
        axis=1,
    )
    facts_in = lax.all_to_all(facts, "expert", split_axis=0, concat_axis=0, tiled=True)
    buffer = jnp.dot(
        filled.astype(jnp.bfloat16), cotangent, preferred_element_type=jnp.float32
    ).astype(cotangent.dtype)
    part = lax.all_to_all(
        buffer.reshape(experts, per_source, width),
        "expert",
        split_axis=0,
        concat_axis=0,
        tiled=True,
    ).reshape(slots, width)
    token_rows = lax.all_gather(part, "tensor", axis=1, tiled=True)
    pick_weight = facts_in[:, :per_source].reshape(slots)
    column_client = jnp.arange(adapter_groups * ADAPTER_RANK, dtype=jnp.int32) // ADAPTER_RANK
    client_mask = (
        facts_in[:, per_source:].reshape(slots, 1) == (column_client + 1).astype(jnp.float32)
    ).astype(jnp.float32)
    act, slope = silu_parts(gate_preactivation[0].astype(jnp.float32))
    up_full = up_preactivation[0].astype(jnp.float32)
    hidden_units = act * up_full
    hidden_lowrank = hidden_units.astype(jnp.bfloat16)
    contract_dims = (((1,), (1,)), ((), ()))
    row_dimensions = (((0,), (0,)), ((), ()))
    frozen_output = lax.dot_general(
        token_rows, down_matrix[0], contract_dims, preferred_element_type=jnp.float32
    )
    projected_piece = (
        jnp.dot(hidden_lowrank, adapter_input_maps[0], preferred_element_type=jnp.float32)
        * client_mask
    )
    local_terms = jnp.sum(hidden_units * frozen_output, axis=1)
    output_map_whole = lax.all_gather(adapter_output_maps[0], "tensor", axis=1, tiled=True)
    adapter_output = (
        lax.dot_general(
            token_rows, output_map_whole, contract_dims, preferred_element_type=jnp.float32
        )
        * client_mask
    )
    projected_rows = lax.psum(projected_piece, "tensor")
    backward_result = lax.dot_general(
        adapter_output.astype(jnp.bfloat16),
        adapter_input_maps[0],
        contract_dims,
        preferred_element_type=jnp.float32,
    )
    hidden_gradient = pick_weight[:, None] * (frozen_output + adapter_scale * backward_result)
    gate_gradient = (hidden_gradient * up_full * slope).astype(jnp.bfloat16)
    up_gradient = (hidden_gradient * act).astype(jnp.bfloat16)
    input_map_gradient = adapter_scale * lax.dot_general(
        hidden_lowrank,
        (pick_weight[:, None] * adapter_output).astype(jnp.bfloat16),
        row_dimensions,
        preferred_element_type=jnp.float32,
    )
    output_map_gradient = adapter_scale * lax.dot_general(
        (pick_weight[:, None] * projected_rows).astype(jnp.bfloat16),
        part,
        row_dimensions,
        preferred_element_type=jnp.float32,
    )
    slot_piece = local_terms + adapter_scale * jnp.sum(projected_piece * adapter_output, axis=1)
    tensors = lax.axis_size("tensor")
    outgoing = jnp.broadcast_to(
        slot_piece.reshape(experts, 1, per_source), (experts, tensors, per_source)
    ).reshape(experts * tensors, per_source)
    returned = lax.all_to_all(
        outgoing, ("expert", "tensor"), split_axis=0, concat_axis=0, tiled=True
    )
    slot_gradient = jnp.sum(returned.reshape(experts, tensors, per_source), axis=1).reshape(-1)
    gate_grad = jnp.stack(
        [
            jnp.sum(jnp.where(chosen[k], slot_gradient[:, None], 0.0), axis=0)
            for k in range(picks_per)
        ],
        axis=1,
    )
    return (
        gate_grad,
        gate_gradient[None],
        up_gradient[None],
        input_map_gradient[None],
        output_map_gradient[None],
    )


def solution(mesh):
    in_specs = (
        P("expert", "tensor"),
        P("expert", None),
        P("expert", None),
        P("expert"),
        P("expert", None, "tensor"),
        P("expert", None, "tensor"),
        P("expert", "tensor", None),
        P("expert", "tensor", None),
        P("expert", None, "tensor"),
    )
    out_specs = (
        P("expert", None),
        P("expert", None, "tensor"),
        P("expert", None, "tensor"),
        P("expert", "tensor", None),
        P("expert", None, "tensor"),
    )
    return jax.shard_map(local, mesh=mesh, in_specs=in_specs, out_specs=out_specs, check_vma=False)
```

```python
import functools

import jax
import jax.numpy as jnp
from jax import lax
from jax.experimental import pallas as pl
from jax.experimental.pallas import tpu as pltpu
from jax.sharding import PartitionSpec as P

ADAPTER_RANK = 16


adapter_scale = 2.0


MESH = pl.DeviceIdType.MESH
TILE_ROWS = 16
LANES = 128


def exchange_kernel(
    experts,
    blocks,
    facts,
    piece,
    maps,
    rows,
    facts_in,
    other_piece,
    maps_whole,
    row_send,
    row_recv,
    fact_send,
    fact_recv,
    pass_send,
    pass_recv,
    pair_send,
    pair_recv,
    own_sem,
):
    expert = lax.axis_index("expert")
    tensor = lax.axis_index("tensor")
    width = blocks.shape[2]
    columns = pl.ds(pl.multiple_of(tensor * width, LANES), width)
    partner = (expert, 1 - tensor)

    barrier = pltpu.get_barrier_semaphore()

    @pl.loop(1, experts)
    def _(step):
        peer = lax.rem(expert + step, experts)
        pl.semaphore_signal(barrier, inc=1, device_id=(peer, tensor), device_id_type=MESH)

    pl.semaphore_signal(barrier, inc=1, device_id=partner, device_id_type=MESH)
    pl.semaphore_wait(barrier, experts)

    def remote(source, target, send, recv, device):
        return pltpu.make_async_remote_copy(
            src_ref=source,
            dst_ref=target,
            send_sem=send,
            recv_sem=recv,
            device_id=device,
            device_id_type=MESH,
        )

    def row_copy(step):
        peer = lax.rem(expert + step, experts)
        return remote(
            blocks.at[peer],
            rows.at[expert, :, columns],
            row_send.at[step],
            row_recv.at[step],
            (peer, tensor),
        )

    def fact_copy(step):
        peer = lax.rem(expert + step, experts)
        return remote(
            facts.at[peer],
            facts_in.at[expert],
            fact_send.at[step],
            fact_recv.at[step],
            (peer, tensor),
        )

    def pass_copy(step):
        source = lax.rem(expert - step + experts, experts)
        return remote(
            rows.at[source, :, columns],
            rows.at[source, :, columns],
            pass_send.at[step],
            pass_recv.at[step],
            partner,
        )

    @pl.loop(1, experts)
    def _(step):
        row_copy(step).start()

    @pl.loop(1, experts)
    def _(step):
        fact_copy(step).start()

    own_copies = [
        pltpu.make_async_copy(blocks.at[expert], rows.at[expert, :, columns], own_sem.at[0]),
        pltpu.make_async_copy(facts.at[expert], facts_in.at[expert], own_sem.at[1]),
        pltpu.make_async_copy(maps, maps_whole.at[:, columns], own_sem.at[2]),
    ]
    pair_copies = [
        remote(piece, other_piece, pair_send.at[0], pair_recv.at[0], partner),
        remote(maps, maps_whole.at[:, columns], pair_send.at[1], pair_recv.at[1], partner),
        remote(
            blocks.at[expert],
            rows.at[expert, :, columns],
            pair_send.at[2],
            pair_recv.at[2],
            partner,
        ),
    ]
    for copy in own_copies + pair_copies:
        copy.start()

    @pl.loop(1, experts)
    def _(step):
        row_copy(step).wait_recv()
        pass_copy(step).start()

    for copy in own_copies + pair_copies:
        copy.wait()

    @pl.loop(1, experts)
    def _(step):
        fact_copy(step).wait()
        row_copy(step).wait_send()
        pass_copy(step).wait()


def exchange(blocks, facts, piece, maps):
    experts, per_source, width = blocks.shape
    anywhere = pl.BlockSpec(memory_space=pl.ANY)
    sems = pltpu.SemaphoreType.DMA
    return pl.pallas_call(
        functools.partial(exchange_kernel, experts),
        out_shape=(
            jax.ShapeDtypeStruct((experts, per_source, 2 * width), blocks.dtype),
            jax.ShapeDtypeStruct(facts.shape, facts.dtype),
            jax.ShapeDtypeStruct(piece.shape, piece.dtype),
            jax.ShapeDtypeStruct((maps.shape[0], 2 * width), maps.dtype),
        ),
        in_specs=[anywhere] * 4,
        out_specs=(anywhere,) * 4,
        scratch_shapes=[sems((experts,))] * 6 + [sems((3,))] * 3,
        compiler_params=pltpu.CompilerParams(collective_id=0, has_side_effects=True),
        name="exchange",
    )(blocks, facts, piece, maps)


def fits_exchange(experts, per_source, width):
    return (
        lax.axis_size("tensor") == 2
        and per_source % TILE_ROWS == 0
        and 2 * per_source <= LANES
        and width % LANES == 0
        and experts > 1
    )


def silu_parts(gate):
    sig = jax.nn.sigmoid(gate)
    return (gate * sig, sig * (1.0 + gate * (1.0 - sig)))


def local(
    cotangent,
    routes,
    router_weight,
    clients,
    gate_preactivation,
    up_preactivation,
    down_matrix,
    adapter_input_maps,
    adapter_output_maps,
):
    experts = lax.axis_size("expert")
    tok_rows = cotangent.shape[0]
    width = cotangent.shape[1]
    picks_per = routes.shape[1]
    slots = gate_preactivation.shape[1]
    per_source = slots // experts
    adapter_groups = adapter_input_maps.shape[2] // ADAPTER_RANK
    token_ids = jnp.arange(tok_rows, dtype=jnp.int32)
    expert_ids = jnp.arange(experts, dtype=jnp.int32)
    slot_ids = jnp.arange(experts * per_source, dtype=jnp.int32)
    hits = (routes[:, :, None] == expert_ids).astype(jnp.float32)
    earlier = (token_ids[:, None] > token_ids[None, :]).astype(jnp.bfloat16)
    before = jnp.dot(
        earlier, jnp.sum(hits, axis=1).astype(jnp.bfloat16), preferred_element_type=jnp.float32
    )
    rank = jnp.sum(before[:, None, :] * hits, axis=2).astype(jnp.int32)
    slot = routes * per_source + rank
    chosen = [slot_ids[:, None] == slot[None, :, k] for k in range(picks_per)]
    filled = functools.reduce(jnp.logical_or, chosen)
    weight_slots = sum(
        jnp.sum(jnp.where(chosen[k], router_weight[None, :, k], 0.0), axis=1)
        for k in range(picks_per)
    )
    client_slots = jnp.sum(
        jnp.where(filled, (clients[None, :] + 1).astype(jnp.float32), 0.0), axis=1
    )
    facts = jnp.concatenate(
        [weight_slots.reshape(experts, per_source), client_slots.reshape(experts, per_source)],
        axis=1,
    )
    buffer = jnp.dot(
        filled.astype(jnp.bfloat16), cotangent, preferred_element_type=jnp.float32
    ).astype(cotangent.dtype)
    act, slope = silu_parts(gate_preactivation[0].astype(jnp.float32))
    up_full = up_preactivation[0].astype(jnp.float32)
    hidden_units = act * up_full
    hidden_lowrank = hidden_units.astype(jnp.bfloat16)
    contract_dims = (((1,), (1,)), ((), ()))
    row_dimensions = (((0,), (0,)), ((), ()))
    unmasked_piece = jnp.dot(
        hidden_lowrank, adapter_input_maps[0], preferred_element_type=jnp.float32
    )
    blocks = buffer.reshape(experts, per_source, width)
    if fits_exchange(experts, per_source, width):
        tiles = jnp.zeros((experts, 8, LANES), jnp.float32)
        tiles = lax.dynamic_update_slice(tiles, facts[:, None, :], (0, 0, 0))
        arrived, tiles_in, other_piece, output_map_whole = exchange(
            blocks, tiles, unmasked_piece, adapter_output_maps[0]
        )
        facts_in = tiles_in[:, 0, : 2 * per_source]
        token_rows = arrived.reshape(slots, 2 * width)
        part = lax.dynamic_slice_in_dim(token_rows, lax.axis_index("tensor") * width, width, 1)
        unmasked_rows = unmasked_piece + other_piece
    else:
        facts_in = lax.all_to_all(facts, "expert", split_axis=0, concat_axis=0, tiled=True)
        part = lax.all_to_all(
            blocks, "expert", split_axis=0, concat_axis=0, tiled=True
        ).reshape(slots, width)
        token_rows = lax.all_gather(part, "tensor", axis=1, tiled=True)
        output_map_whole = lax.all_gather(adapter_output_maps[0], "tensor", axis=1, tiled=True)
        unmasked_rows = lax.psum(unmasked_piece, "tensor")
    pick_weight = facts_in[:, :per_source].reshape(slots)
    column_client = jnp.arange(adapter_groups * ADAPTER_RANK, dtype=jnp.int32) // ADAPTER_RANK
    client_mask = (
        facts_in[:, per_source:].reshape(slots, 1) == (column_client + 1).astype(jnp.float32)
    ).astype(jnp.float32)
    frozen_output = lax.dot_general(
        token_rows, down_matrix[0], contract_dims, preferred_element_type=jnp.float32
    )
    projected_piece = unmasked_piece * client_mask
    projected_rows = unmasked_rows * client_mask
    local_terms = jnp.sum(hidden_units * frozen_output, axis=1)
    adapter_output = (
        lax.dot_general(
            token_rows, output_map_whole, contract_dims, preferred_element_type=jnp.float32
        )
        * client_mask
    )
    backward_result = lax.dot_general(
        adapter_output.astype(jnp.bfloat16),
        adapter_input_maps[0],
        contract_dims,
        preferred_element_type=jnp.float32,
    )
    hidden_gradient = pick_weight[:, None] * (frozen_output + adapter_scale * backward_result)
    gate_gradient = (hidden_gradient * up_full * slope).astype(jnp.bfloat16)
    up_gradient = (hidden_gradient * act).astype(jnp.bfloat16)
    input_map_gradient = adapter_scale * lax.dot_general(
        hidden_lowrank,
        (pick_weight[:, None] * adapter_output).astype(jnp.bfloat16),
        row_dimensions,
        preferred_element_type=jnp.float32,
    )
    output_map_gradient = adapter_scale * lax.dot_general(
        (pick_weight[:, None] * projected_rows).astype(jnp.bfloat16),
        part,
        row_dimensions,
        preferred_element_type=jnp.float32,
    )
    slot_piece = local_terms + adapter_scale * jnp.sum(projected_piece * adapter_output, axis=1)
    tensors = lax.axis_size("tensor")
    outgoing = jnp.broadcast_to(
        slot_piece.reshape(experts, 1, per_source), (experts, tensors, per_source)
    ).reshape(experts * tensors, per_source)
    returned = lax.all_to_all(
        outgoing, ("expert", "tensor"), split_axis=0, concat_axis=0, tiled=True
    )
    slot_gradient = jnp.sum(returned.reshape(experts, tensors, per_source), axis=1).reshape(-1)
    gate_grad = jnp.stack(
        [
            jnp.sum(jnp.where(chosen[k], slot_gradient[:, None], 0.0), axis=0)
            for k in range(picks_per)
        ],
        axis=1,
    )
    return (
        gate_grad,
        gate_gradient[None],
        up_gradient[None],
        input_map_gradient[None],
        output_map_gradient[None],
    )


def solution(mesh):
    in_specs = (
        P("expert", "tensor"),
        P("expert", None),
        P("expert", None),
        P("expert"),
        P("expert", None, "tensor"),
        P("expert", None, "tensor"),
        P("expert", "tensor", None),
        P("expert", "tensor", None),
        P("expert", None, "tensor"),
    )
    out_specs = (
        P("expert", None),
        P("expert", None, "tensor"),
        P("expert", None, "tensor"),
        P("expert", "tensor", None),
        P("expert", None, "tensor"),
    )
    return jax.shard_map(local, mesh=mesh, in_specs=in_specs, out_specs=out_specs, check_vma=False)
```

```python
import functools

import jax
import jax.numpy as jnp
from jax import lax
from jax.experimental import pallas as pl
from jax.experimental.pallas import tpu as pltpu
from jax.sharding import PartitionSpec as P

ADAPTER_RANK = 16


adapter_scale = 2.0


MESH = pl.DeviceIdType.MESH
TILE_ROWS = 16
LANES = 128
UNIT_TILE = 256
VMEM_BYTES = 40 * 1024 * 1024


def exchange_kernel(
    experts,
    blocks,
    facts,
    gate,
    up,
    input_maps,
    maps,
    rows,
    facts_in,
    piece,
    other_piece,
    maps_whole,
    row_send,
    row_recv,
    fact_send,
    fact_recv,
    pass_send,
    pass_recv,
    pair_send,
    pair_recv,
    own_sem,
):
    expert = lax.axis_index("expert")
    tensor = lax.axis_index("tensor")
    width = blocks.shape[2]
    columns = pl.ds(pl.multiple_of(tensor * width, LANES), width)
    partner = (expert, 1 - tensor)

    barrier = pltpu.get_barrier_semaphore()

    @pl.loop(1, experts)
    def _(step):
        peer = lax.rem(expert + step, experts)
        pl.semaphore_signal(barrier, inc=1, device_id=(peer, tensor), device_id_type=MESH)

    pl.semaphore_signal(barrier, inc=1, device_id=partner, device_id_type=MESH)
    pl.semaphore_wait(barrier, experts)

    def remote(source, target, send, recv, device):
        return pltpu.make_async_remote_copy(
            src_ref=source,
            dst_ref=target,
            send_sem=send,
            recv_sem=recv,
            device_id=device,
            device_id_type=MESH,
        )

    def row_copy(step):
        peer = lax.rem(expert + step, experts)
        return remote(
            blocks.at[peer],
            rows.at[expert, :, columns],
            row_send.at[step],
            row_recv.at[step],
            (peer, tensor),
        )

    def fact_copy(step):
        peer = lax.rem(expert + step, experts)
        return remote(
            facts.at[peer],
            facts_in.at[expert],
            fact_send.at[step],
            fact_recv.at[step],
            (peer, tensor),
        )

    def pass_copy(step):
        source = lax.rem(expert - step + experts, experts)
        return remote(
            rows.at[source, :, columns],
            rows.at[source, :, columns],
            pass_send.at[step],
            pass_recv.at[step],
            partner,
        )

    @pl.loop(1, experts)
    def _(step):
        row_copy(step).start()

    @pl.loop(1, experts)
    def _(step):
        fact_copy(step).start()

    own_copies = [
        pltpu.make_async_copy(blocks.at[expert], rows.at[expert, :, columns], own_sem.at[0]),
        pltpu.make_async_copy(facts.at[expert], facts_in.at[expert], own_sem.at[1]),
        pltpu.make_async_copy(maps, maps_whole.at[:, columns], own_sem.at[2]),
    ]
    piece_copy = remote(piece, other_piece, pair_send.at[0], pair_recv.at[0], partner)
    pair_copies = [
        remote(maps, maps_whole.at[:, columns], pair_send.at[1], pair_recv.at[1], partner),
        remote(
            blocks.at[expert],
            rows.at[expert, :, columns],
            pair_send.at[2],
            pair_recv.at[2],
            partner,
        ),
    ]
    for copy in own_copies + pair_copies:
        copy.start()

    part_rows = gate.shape[0] // 4

    @pl.loop(0, 4)
    def _(index):
        span = pl.ds(pl.multiple_of(index * part_rows, part_rows), part_rows)
        hidden = silu_parts(gate[span, :].astype(jnp.float32))[0] * up[span, :].astype(jnp.float32)
        piece[span, :] = jnp.dot(
            hidden.astype(jnp.bfloat16), input_maps[...], preferred_element_type=jnp.float32
        )

    piece_copy.start()

    @pl.loop(1, experts)
    def _(step):
        row_copy(step).wait_recv()
        pass_copy(step).start()

    for copy in own_copies + pair_copies + [piece_copy]:
        copy.wait()

    @pl.loop(1, experts)
    def _(step):
        fact_copy(step).wait()
        row_copy(step).wait_send()
        pass_copy(step).wait()


def exchange(blocks, facts, gate, up, input_maps, maps):
    experts, per_source, width = blocks.shape
    anywhere = pl.BlockSpec(memory_space=pl.ANY)
    vmem = pl.BlockSpec(memory_space=pltpu.VMEM)
    sems = pltpu.SemaphoreType.DMA
    return pl.pallas_call(
        functools.partial(exchange_kernel, experts),
        out_shape=(
            jax.ShapeDtypeStruct((experts, per_source, 2 * width), blocks.dtype),
            jax.ShapeDtypeStruct(facts.shape, facts.dtype),
            jax.ShapeDtypeStruct((gate.shape[0], input_maps.shape[1]), jnp.float32),
            jax.ShapeDtypeStruct((gate.shape[0], input_maps.shape[1]), jnp.float32),
            jax.ShapeDtypeStruct((maps.shape[0], 2 * width), maps.dtype),
        ),
        in_specs=[anywhere] * 2 + [vmem] * 3 + [anywhere],
        out_specs=(anywhere, anywhere, vmem, anywhere, anywhere),
        scratch_shapes=[sems((experts,))] * 6 + [sems((3,))] * 3,
        compiler_params=pltpu.CompilerParams(
            collective_id=0, has_side_effects=True, vmem_limit_bytes=VMEM_BYTES
        ),
        name="exchange",
    )(blocks, facts, gate, up, input_maps, maps)


def gradients_kernel(
    rows,
    maps,
    down,
    input_maps,
    gate,
    up,
    weight,
    mask,
    piece,
    other_piece,
    gate_out,
    up_out,
    input_out,
    output_out,
    slot_out,
    adapter,
):
    contract_dims = (((1,), (1,)), ((), ()))
    row_dimensions = (((0,), (0,)), ((), ()))

    @pl.when(pl.program_id(0) == 0)
    def _():
        adapter[...] = (
            lax.dot_general(
                rows[...], maps[...], contract_dims, preferred_element_type=jnp.float32
            )
            * mask[...]
        )
        projected = (piece[...] + other_piece[...]) * mask[...]
        width = output_out.shape[1]
        columns = pl.ds(pl.multiple_of(lax.axis_index("tensor") * width, LANES), width)
        output_out[...] = adapter_scale * lax.dot_general(
            (weight[...] * projected).astype(jnp.bfloat16),
            rows[:, columns],
            row_dimensions,
            preferred_element_type=jnp.float32,
        )
        slot_out[...] = adapter_scale * jnp.sum(
            piece[...] * mask[...] * adapter[...], axis=1, keepdims=True
        )

    base = lax.dot_general(rows[...], down[...], contract_dims, preferred_element_type=jnp.float32)
    act, slope = silu_parts(gate[...].astype(jnp.float32))
    up_full = up[...].astype(jnp.float32)
    hidden = act * up_full
    slot_out[...] += jnp.sum(hidden * base, axis=1, keepdims=True)
    backward = lax.dot_general(
        adapter[...].astype(jnp.bfloat16),
        input_maps[...],
        contract_dims,
        preferred_element_type=jnp.float32,
    )
    hidden_gradient = weight[...] * (base + adapter_scale * backward)
    gate_out[...] = (hidden_gradient * up_full * slope).astype(jnp.bfloat16)
    up_out[...] = (hidden_gradient * act).astype(jnp.bfloat16)
    input_out[...] = adapter_scale * lax.dot_general(
        hidden.astype(jnp.bfloat16),
        (weight[...] * adapter[...]).astype(jnp.bfloat16),
        row_dimensions,
        preferred_element_type=jnp.float32,
    )


def gradients(rows, maps, down, input_maps, gate, up, weight, mask, piece, other_piece):
    slots, full = rows.shape
    units = gate.shape[1]
    columns = maps.shape[0]
    tile = UNIT_TILE if units % UNIT_TILE == 0 else LANES

    def whole(array):
        return pl.BlockSpec(array.shape, lambda step: (0, 0))

    by_unit = pl.BlockSpec((slots, tile), lambda step: (0, step))
    by_row = pl.BlockSpec((tile, columns), lambda step: (step, 0))
    output_out = jax.ShapeDtypeStruct((columns, full // 2), jnp.float32)
    slot_out = jax.ShapeDtypeStruct((slots, 1), jnp.float32)
    return pl.pallas_call(
        gradients_kernel,
        grid=(units // tile,),
        in_specs=[
            whole(rows),
            whole(maps),
            pl.BlockSpec((tile, full), lambda step: (step, 0)),
            by_row,
            by_unit,
            by_unit,
            whole(weight),
            whole(mask),
            whole(piece),
            whole(other_piece),
        ],
        out_specs=(by_unit, by_unit, by_row, whole(output_out), whole(slot_out)),
        out_shape=(
            jax.ShapeDtypeStruct(gate.shape, jnp.bfloat16),
            jax.ShapeDtypeStruct(gate.shape, jnp.bfloat16),
            jax.ShapeDtypeStruct(input_maps.shape, jnp.float32),
            output_out,
            slot_out,
        ),
        scratch_shapes=[pltpu.VMEM((slots, columns), jnp.float32)],
        compiler_params=pltpu.CompilerParams(vmem_limit_bytes=VMEM_BYTES),
        name="gradients",
    )(rows, maps, down, input_maps, gate, up, weight, mask, piece, other_piece)


def fits_exchange(experts, per_source, width, units):
    return (
        lax.axis_size("tensor") == 2
        and per_source % TILE_ROWS == 0
        and 2 * per_source <= LANES
        and width % LANES == 0
        and units % LANES == 0
        and experts > 1
    )


def silu_parts(gate):
    sig = jax.nn.sigmoid(gate)
    return (gate * sig, sig * (1.0 + gate * (1.0 - sig)))


def local(
    cotangent,
    routes,
    router_weight,
    clients,
    gate_preactivation,
    up_preactivation,
    down_matrix,
    adapter_input_maps,
    adapter_output_maps,
):
    experts = lax.axis_size("expert")
    tok_rows = cotangent.shape[0]
    width = cotangent.shape[1]
    picks_per = routes.shape[1]
    slots = gate_preactivation.shape[1]
    per_source = slots // experts
    adapter_groups = adapter_input_maps.shape[2] // ADAPTER_RANK
    token_ids = jnp.arange(tok_rows, dtype=jnp.int32)
    expert_ids = jnp.arange(experts, dtype=jnp.int32)
    slot_ids = jnp.arange(experts * per_source, dtype=jnp.int32)
    hits = (routes[:, :, None] == expert_ids).astype(jnp.float32)
    earlier = (token_ids[:, None] > token_ids[None, :]).astype(jnp.bfloat16)
    before = jnp.dot(
        earlier, jnp.sum(hits, axis=1).astype(jnp.bfloat16), preferred_element_type=jnp.float32
    )
    rank = jnp.sum(before[:, None, :] * hits, axis=2).astype(jnp.int32)
    slot = routes * per_source + rank
    chosen = [slot_ids[:, None] == slot[None, :, k] for k in range(picks_per)]
    filled = functools.reduce(jnp.logical_or, chosen)
    weight_slots = sum(
        jnp.sum(jnp.where(chosen[k], router_weight[None, :, k], 0.0), axis=1)
        for k in range(picks_per)
    )
    client_slots = jnp.sum(
        jnp.where(filled, (clients[None, :] + 1).astype(jnp.float32), 0.0), axis=1
    )
    facts = jnp.concatenate(
        [weight_slots.reshape(experts, per_source), client_slots.reshape(experts, per_source)],
        axis=1,
    )
    buffer = jnp.dot(
        filled.astype(jnp.bfloat16), cotangent, preferred_element_type=jnp.float32
    ).astype(cotangent.dtype)
    blocks = buffer.reshape(experts, per_source, width)
    column_client = jnp.arange(adapter_groups * ADAPTER_RANK, dtype=jnp.int32) // ADAPTER_RANK

    def slot_facts(facts_in):
        client = facts_in[:, per_source:].reshape(slots, 1)
        client_mask = (client == (column_client + 1).astype(jnp.float32)).astype(jnp.float32)
        return facts_in[:, :per_source].reshape(slots, 1), client_mask

    if fits_exchange(experts, per_source, width, gate_preactivation.shape[2]):
        tiles = jnp.zeros((experts, 8, LANES), jnp.float32)
        tiles = lax.dynamic_update_slice(tiles, facts[:, None, :], (0, 0, 0))
        arrived, tiles_in, piece, other_piece, output_map_whole = exchange(
            blocks,
            tiles,
            gate_preactivation[0],
            up_preactivation[0],
            adapter_input_maps[0],
            adapter_output_maps[0],
        )
        pick_weight, client_mask = slot_facts(tiles_in[:, 0, : 2 * per_source])
        gate_gradient, up_gradient, input_map_gradient, output_map_gradient, slot_piece = gradients(
            arrived.reshape(slots, 2 * width),
            output_map_whole,
            down_matrix[0],
            adapter_input_maps[0],
            gate_preactivation[0],
            up_preactivation[0],
            pick_weight,
            client_mask,
            piece,
            other_piece,
        )
    else:
        act, slope = silu_parts(gate_preactivation[0].astype(jnp.float32))
        up_full = up_preactivation[0].astype(jnp.float32)
        hidden_units = act * up_full
        hidden_lowrank = hidden_units.astype(jnp.bfloat16)
        contract_dims = (((1,), (1,)), ((), ()))
        row_dimensions = (((0,), (0,)), ((), ()))
        unmasked_piece = jnp.dot(
            hidden_lowrank, adapter_input_maps[0], preferred_element_type=jnp.float32
        )
        facts_in = lax.all_to_all(facts, "expert", split_axis=0, concat_axis=0, tiled=True)
        part = lax.all_to_all(
            blocks, "expert", split_axis=0, concat_axis=0, tiled=True
        ).reshape(slots, width)
        token_rows = lax.all_gather(part, "tensor", axis=1, tiled=True)
        output_map_whole = lax.all_gather(adapter_output_maps[0], "tensor", axis=1, tiled=True)
        unmasked_rows = lax.psum(unmasked_piece, "tensor")
        pick_weight, client_mask = slot_facts(facts_in)
        frozen_output = lax.dot_general(
            token_rows, down_matrix[0], contract_dims, preferred_element_type=jnp.float32
        )
        projected_piece = unmasked_piece * client_mask
        projected_rows = unmasked_rows * client_mask
        local_terms = jnp.sum(hidden_units * frozen_output, axis=1)
        adapter_output = (
            lax.dot_general(
                token_rows, output_map_whole, contract_dims, preferred_element_type=jnp.float32
            )
            * client_mask
        )
        backward_result = lax.dot_general(
            adapter_output.astype(jnp.bfloat16),
            adapter_input_maps[0],
            contract_dims,
            preferred_element_type=jnp.float32,
        )
        hidden_gradient = pick_weight * (frozen_output + adapter_scale * backward_result)
        gate_gradient = (hidden_gradient * up_full * slope).astype(jnp.bfloat16)
        up_gradient = (hidden_gradient * act).astype(jnp.bfloat16)
        input_map_gradient = adapter_scale * lax.dot_general(
            hidden_lowrank,
            (pick_weight * adapter_output).astype(jnp.bfloat16),
            row_dimensions,
            preferred_element_type=jnp.float32,
        )
        output_map_gradient = adapter_scale * lax.dot_general(
            (pick_weight * projected_rows).astype(jnp.bfloat16),
            part,
            row_dimensions,
            preferred_element_type=jnp.float32,
        )
        slot_piece = local_terms + adapter_scale * jnp.sum(projected_piece * adapter_output, axis=1)
    tensors = lax.axis_size("tensor")
    outgoing = jnp.broadcast_to(
        slot_piece.reshape(experts, 1, per_source), (experts, tensors, per_source)
    ).reshape(experts * tensors, per_source)
    returned = lax.all_to_all(
        outgoing, ("expert", "tensor"), split_axis=0, concat_axis=0, tiled=True
    )
    slot_gradient = jnp.sum(returned.reshape(experts, tensors, per_source), axis=1).reshape(-1)
    gate_grad = jnp.stack(
        [
            jnp.sum(jnp.where(chosen[k], slot_gradient[:, None], 0.0), axis=0)
            for k in range(picks_per)
        ],
        axis=1,
    )
    return (
        gate_grad,
        gate_gradient[None],
        up_gradient[None],
        input_map_gradient[None],
        output_map_gradient[None],
    )


def solution(mesh):
    in_specs = (
        P("expert", "tensor"),
        P("expert", None),
        P("expert", None),
        P("expert"),
        P("expert", None, "tensor"),
        P("expert", None, "tensor"),
        P("expert", "tensor", None),
        P("expert", "tensor", None),
        P("expert", None, "tensor"),
    )
    out_specs = (
        P("expert", None),
        P("expert", None, "tensor"),
        P("expert", None, "tensor"),
        P("expert", "tensor", None),
        P("expert", None, "tensor"),
    )
    return jax.shard_map(local, mesh=mesh, in_specs=in_specs, out_specs=out_specs, check_vma=False)
```

```python
import functools

import jax
import jax.numpy as jnp
from jax import lax
from jax.experimental import pallas as pl
from jax.experimental.pallas import tpu as pltpu
from jax.sharding import PartitionSpec as P

ADAPTER_RANK = 16


adapter_scale = 2.0


MESH = pl.DeviceIdType.MESH
TILE_ROWS = 16
LANES = 128
UNIT_TILE = 256
VMEM_BYTES = 60 * 1024 * 1024


def exchange_kernel(
    experts,
    blocks,
    facts,
    gate,
    up,
    input_maps,
    maps,
    rows,
    facts_in,
    piece,
    other_piece,
    maps_whole,
    row_send,
    row_recv,
    fact_send,
    fact_recv,
    pass_send,
    pass_recv,
    pair_send,
    pair_recv,
    own_sem,
):
    expert = lax.axis_index("expert")
    tensor = lax.axis_index("tensor")
    width = blocks.shape[2]
    columns = pl.ds(pl.multiple_of(tensor * width, LANES), width)
    partner = (expert, 1 - tensor)

    barrier = pltpu.get_barrier_semaphore()

    @pl.loop(1, experts)
    def _(step):
        peer = lax.rem(expert + step, experts)
        pl.semaphore_signal(barrier, inc=1, device_id=(peer, tensor), device_id_type=MESH)

    pl.semaphore_signal(barrier, inc=1, device_id=partner, device_id_type=MESH)
    pl.semaphore_wait(barrier, experts)

    def remote(source, target, send, recv, device):
        return pltpu.make_async_remote_copy(
            src_ref=source,
            dst_ref=target,
            send_sem=send,
            recv_sem=recv,
            device_id=device,
            device_id_type=MESH,
        )

    def row_copy(step):
        peer = lax.rem(expert + step, experts)
        return remote(
            blocks.at[peer],
            rows.at[expert, :, columns],
            row_send.at[step],
            row_recv.at[step],
            (peer, tensor),
        )

    def fact_copy(step):
        peer = lax.rem(expert + step, experts)
        return remote(
            facts.at[peer],
            facts_in.at[expert],
            fact_send.at[step],
            fact_recv.at[step],
            (peer, tensor),
        )

    def pass_copy(step):
        source = lax.rem(expert - step + experts, experts)
        return remote(
            rows.at[source, :, columns],
            rows.at[source, :, columns],
            pass_send.at[step],
            pass_recv.at[step],
            partner,
        )

    @pl.loop(1, experts)
    def _(step):
        row_copy(step).start()

    @pl.loop(1, experts)
    def _(step):
        fact_copy(step).start()

    own_copies = [
        pltpu.make_async_copy(blocks.at[expert], rows.at[expert, :, columns], own_sem.at[0]),
        pltpu.make_async_copy(facts.at[expert], facts_in.at[expert], own_sem.at[1]),
        pltpu.make_async_copy(maps, maps_whole.at[:, columns], own_sem.at[2]),
    ]
    piece_copy = remote(piece, other_piece, pair_send.at[0], pair_recv.at[0], partner)
    pair_copies = [
        remote(maps, maps_whole.at[:, columns], pair_send.at[1], pair_recv.at[1], partner),
        remote(
            blocks.at[expert],
            rows.at[expert, :, columns],
            pair_send.at[2],
            pair_recv.at[2],
            partner,
        ),
    ]
    for copy in own_copies + pair_copies:
        copy.start()

    part_rows = gate.shape[0] // 4

    @pl.loop(0, 4)
    def _(index):
        span = pl.ds(pl.multiple_of(index * part_rows, part_rows), part_rows)
        hidden = silu_parts(gate[span, :].astype(jnp.float32))[0] * up[span, :].astype(jnp.float32)
        piece[span, :] = jnp.dot(
            hidden.astype(jnp.bfloat16), input_maps[...], preferred_element_type=jnp.float32
        )

    piece_copy.start()

    @pl.loop(1, experts)
    def _(step):
        row_copy(step).wait_recv()
        pass_copy(step).start()

    for copy in own_copies + pair_copies + [piece_copy]:
        copy.wait()

    @pl.loop(1, experts)
    def _(step):
        fact_copy(step).wait()
        row_copy(step).wait_send()
        pass_copy(step).wait()


def exchange(blocks, facts, gate, up, input_maps, maps):
    experts, per_source, width = blocks.shape
    anywhere = pl.BlockSpec(memory_space=pl.ANY)
    vmem = pl.BlockSpec(memory_space=pltpu.VMEM)
    sems = pltpu.SemaphoreType.DMA
    return pl.pallas_call(
        functools.partial(exchange_kernel, experts),
        out_shape=(
            jax.ShapeDtypeStruct((experts, per_source, 2 * width), blocks.dtype),
            jax.ShapeDtypeStruct(facts.shape, facts.dtype),
            jax.ShapeDtypeStruct((gate.shape[0], input_maps.shape[1]), jnp.float32),
            jax.ShapeDtypeStruct((gate.shape[0], input_maps.shape[1]), jnp.float32),
            jax.ShapeDtypeStruct((maps.shape[0], 2 * width), maps.dtype),
        ),
        in_specs=[anywhere] * 2 + [vmem] * 3 + [anywhere],
        out_specs=(anywhere, anywhere, vmem, anywhere, anywhere),
        scratch_shapes=[sems((experts,))] * 6 + [sems((3,))] * 3,
        compiler_params=pltpu.CompilerParams(
            collective_id=0, has_side_effects=True, vmem_limit_bytes=VMEM_BYTES
        ),
        name="exchange",
    )(blocks, facts, gate, up, input_maps, maps)


def gradients_kernel(
    rows,
    maps,
    down,
    input_maps,
    gate,
    up,
    weight,
    mask,
    piece,
    other_piece,
    gate_out,
    up_out,
    input_out,
    output_out,
    slot_out,
    adapter,
):
    contract_dims = (((1,), (1,)), ((), ()))
    row_dimensions = (((0,), (0,)), ((), ()))

    @pl.when(pl.program_id(0) == 0)
    def _():
        adapter[...] = (
            lax.dot_general(
                rows[...], maps[...], contract_dims, preferred_element_type=jnp.float32
            )
            * mask[...]
        )
        projected = (piece[...] + other_piece[...]) * mask[...]
        width = output_out.shape[1]
        columns = pl.ds(pl.multiple_of(lax.axis_index("tensor") * width, LANES), width)
        output_out[...] = adapter_scale * lax.dot_general(
            (weight[...] * projected).astype(jnp.bfloat16),
            rows[:, columns],
            row_dimensions,
            preferred_element_type=jnp.float32,
        )
        slot_out[...] = adapter_scale * jnp.sum(
            piece[...] * mask[...] * adapter[...], axis=1, keepdims=True
        )

    base = lax.dot_general(rows[...], down[...], contract_dims, preferred_element_type=jnp.float32)
    act, slope = silu_parts(gate[...].astype(jnp.float32))
    up_full = up[...].astype(jnp.float32)
    hidden = act * up_full
    slot_out[...] += jnp.sum(hidden * base, axis=1, keepdims=True)
    backward = lax.dot_general(
        adapter[...].astype(jnp.bfloat16),
        input_maps[...],
        contract_dims,
        preferred_element_type=jnp.float32,
    )
    hidden_gradient = weight[...] * (base + adapter_scale * backward)
    gate_out[...] = (hidden_gradient * up_full * slope).astype(jnp.bfloat16)
    up_out[...] = (hidden_gradient * act).astype(jnp.bfloat16)
    input_out[...] = adapter_scale * lax.dot_general(
        hidden.astype(jnp.bfloat16),
        (weight[...] * adapter[...]).astype(jnp.bfloat16),
        row_dimensions,
        preferred_element_type=jnp.float32,
    )


def gradients(rows, maps, down, input_maps, gate, up, weight, mask, piece, other_piece):
    slots, full = rows.shape
    units = gate.shape[1]
    columns = maps.shape[0]
    tile = UNIT_TILE if units % UNIT_TILE == 0 else LANES

    def whole(array):
        return pl.BlockSpec(array.shape, lambda step: (0, 0))

    by_unit = pl.BlockSpec((slots, tile), lambda step: (0, step))
    by_row = pl.BlockSpec((tile, columns), lambda step: (step, 0))
    output_out = jax.ShapeDtypeStruct((columns, full // 2), jnp.float32)
    slot_out = jax.ShapeDtypeStruct((slots, 1), jnp.float32)
    return pl.pallas_call(
        gradients_kernel,
        grid=(units // tile,),
        in_specs=[
            whole(rows),
            whole(maps),
            pl.BlockSpec((tile, full), lambda step: (step, 0)),
            by_row,
            by_unit,
            by_unit,
            whole(weight),
            whole(mask),
            whole(piece),
            whole(other_piece),
        ],
        out_specs=(by_unit, by_unit, by_row, whole(output_out), whole(slot_out)),
        out_shape=(
            jax.ShapeDtypeStruct(gate.shape, jnp.bfloat16),
            jax.ShapeDtypeStruct(gate.shape, jnp.bfloat16),
            jax.ShapeDtypeStruct(input_maps.shape, jnp.float32),
            output_out,
            slot_out,
        ),
        scratch_shapes=[pltpu.VMEM((slots, columns), jnp.float32)],
        compiler_params=pltpu.CompilerParams(vmem_limit_bytes=VMEM_BYTES),
        name="gradients",
    )(rows, maps, down, input_maps, gate, up, weight, mask, piece, other_piece)


def fits_exchange(experts, per_source, width, units):
    return (
        lax.axis_size("tensor") == 2
        and per_source % TILE_ROWS == 0
        and 2 * per_source <= LANES
        and width % LANES == 0
        and units % LANES == 0
        and experts > 1
    )


def silu_parts(gate):
    sig = jax.nn.sigmoid(gate)
    return (gate * sig, sig * (1.0 + gate * (1.0 - sig)))


def local(
    cotangent,
    routes,
    router_weight,
    clients,
    gate_preactivation,
    up_preactivation,
    down_matrix,
    adapter_input_maps,
    adapter_output_maps,
):
    experts = lax.axis_size("expert")
    tok_rows = cotangent.shape[0]
    width = cotangent.shape[1]
    picks_per = routes.shape[1]
    slots = gate_preactivation.shape[1]
    per_source = slots // experts
    adapter_groups = adapter_input_maps.shape[2] // ADAPTER_RANK
    token_ids = jnp.arange(tok_rows, dtype=jnp.int32)
    expert_ids = jnp.arange(experts, dtype=jnp.int32)
    slot_ids = jnp.arange(experts * per_source, dtype=jnp.int32)
    hits = (routes[:, :, None] == expert_ids).astype(jnp.float32)
    earlier = (token_ids[:, None] > token_ids[None, :]).astype(jnp.bfloat16)
    before = jnp.dot(
        earlier, jnp.sum(hits, axis=1).astype(jnp.bfloat16), preferred_element_type=jnp.float32
    )
    rank = jnp.sum(before[:, None, :] * hits, axis=2).astype(jnp.int32)
    slot = routes * per_source + rank
    chosen = [slot_ids[:, None] == slot[None, :, k] for k in range(picks_per)]
    filled = functools.reduce(jnp.logical_or, chosen)
    weight_slots = sum(
        jnp.sum(jnp.where(chosen[k], router_weight[None, :, k], 0.0), axis=1)
        for k in range(picks_per)
    )
    client_slots = jnp.sum(
        jnp.where(filled, (clients[None, :] + 1).astype(jnp.float32), 0.0), axis=1
    )
    facts = jnp.concatenate(
        [weight_slots.reshape(experts, per_source), client_slots.reshape(experts, per_source)],
        axis=1,
    )
    buffer = jnp.dot(
        filled.astype(jnp.bfloat16), cotangent, preferred_element_type=jnp.float32
    ).astype(cotangent.dtype)
    blocks = buffer.reshape(experts, per_source, width)
    column_client = jnp.arange(adapter_groups * ADAPTER_RANK, dtype=jnp.int32) // ADAPTER_RANK

    def slot_facts(facts_in):
        client = facts_in[:, per_source:].reshape(slots, 1)
        client_mask = (client == (column_client + 1).astype(jnp.float32)).astype(jnp.float32)
        return facts_in[:, :per_source].reshape(slots, 1), client_mask

    if fits_exchange(experts, per_source, width, gate_preactivation.shape[2]):
        tiles = jnp.zeros((experts, 8, LANES), jnp.float32)
        tiles = lax.dynamic_update_slice(tiles, facts[:, None, :], (0, 0, 0))
        arrived, tiles_in, piece, other_piece, output_map_whole = exchange(
            blocks,
            tiles,
            gate_preactivation[0],
            up_preactivation[0],
            adapter_input_maps[0],
            adapter_output_maps[0],
        )
        pick_weight, client_mask = slot_facts(tiles_in[:, 0, : 2 * per_source])
        gate_gradient, up_gradient, input_map_gradient, output_map_gradient, slot_piece = gradients(
            arrived.reshape(slots, 2 * width),
            output_map_whole,
            down_matrix[0],
            adapter_input_maps[0],
            gate_preactivation[0],
            up_preactivation[0],
            pick_weight,
            client_mask,
            piece,
            other_piece,
        )
    else:
        act, slope = silu_parts(gate_preactivation[0].astype(jnp.float32))
        up_full = up_preactivation[0].astype(jnp.float32)
        hidden_units = act * up_full
        hidden_lowrank = hidden_units.astype(jnp.bfloat16)
        contract_dims = (((1,), (1,)), ((), ()))
        row_dimensions = (((0,), (0,)), ((), ()))
        unmasked_piece = jnp.dot(
            hidden_lowrank, adapter_input_maps[0], preferred_element_type=jnp.float32
        )
        facts_in = lax.all_to_all(facts, "expert", split_axis=0, concat_axis=0, tiled=True)
        part = lax.all_to_all(
            blocks, "expert", split_axis=0, concat_axis=0, tiled=True
        ).reshape(slots, width)
        token_rows = lax.all_gather(part, "tensor", axis=1, tiled=True)
        output_map_whole = lax.all_gather(adapter_output_maps[0], "tensor", axis=1, tiled=True)
        unmasked_rows = lax.psum(unmasked_piece, "tensor")
        pick_weight, client_mask = slot_facts(facts_in)
        frozen_output = lax.dot_general(
            token_rows, down_matrix[0], contract_dims, preferred_element_type=jnp.float32
        )
        projected_piece = unmasked_piece * client_mask
        projected_rows = unmasked_rows * client_mask
        local_terms = jnp.sum(hidden_units * frozen_output, axis=1)
        adapter_output = (
            lax.dot_general(
                token_rows, output_map_whole, contract_dims, preferred_element_type=jnp.float32
            )
            * client_mask
        )
        backward_result = lax.dot_general(
            adapter_output.astype(jnp.bfloat16),
            adapter_input_maps[0],
            contract_dims,
            preferred_element_type=jnp.float32,
        )
        hidden_gradient = pick_weight * (frozen_output + adapter_scale * backward_result)
        gate_gradient = (hidden_gradient * up_full * slope).astype(jnp.bfloat16)
        up_gradient = (hidden_gradient * act).astype(jnp.bfloat16)
        input_map_gradient = adapter_scale * lax.dot_general(
            hidden_lowrank,
            (pick_weight * adapter_output).astype(jnp.bfloat16),
            row_dimensions,
            preferred_element_type=jnp.float32,
        )
        output_map_gradient = adapter_scale * lax.dot_general(
            (pick_weight * projected_rows).astype(jnp.bfloat16),
            part,
            row_dimensions,
            preferred_element_type=jnp.float32,
        )
        slot_piece = local_terms + adapter_scale * jnp.sum(projected_piece * adapter_output, axis=1)
    tensors = lax.axis_size("tensor")
    outgoing = jnp.broadcast_to(
        slot_piece.reshape(experts, 1, per_source), (experts, tensors, per_source)
    ).reshape(experts * tensors, per_source)
    returned = lax.all_to_all(
        outgoing, ("expert", "tensor"), split_axis=0, concat_axis=0, tiled=True
    )
    slot_gradient = jnp.sum(returned.reshape(experts, tensors, per_source), axis=1).reshape(-1)
    gate_grad = jnp.stack(
        [
            jnp.sum(jnp.where(chosen[k], slot_gradient[:, None], 0.0), axis=0)
            for k in range(picks_per)
        ],
        axis=1,
    )
    return (
        gate_grad,
        gate_gradient[None],
        up_gradient[None],
        input_map_gradient[None],
        output_map_gradient[None],
    )


def solution(mesh):
    in_specs = (
        P("expert", "tensor"),
        P("expert", None),
        P("expert", None),
        P("expert"),
        P("expert", None, "tensor"),
        P("expert", None, "tensor"),
        P("expert", "tensor", None),
        P("expert", "tensor", None),
        P("expert", None, "tensor"),
    )
    out_specs = (
        P("expert", None),
        P("expert", None, "tensor"),
        P("expert", None, "tensor"),
        P("expert", "tensor", None),
        P("expert", None, "tensor"),
    )
    return jax.shard_map(local, mesh=mesh, in_specs=in_specs, out_specs=out_specs, check_vma=False)
```

```python
import functools

import jax
import jax.numpy as jnp
from jax import lax
from jax.experimental import pallas as pl
from jax.experimental.pallas import tpu as pltpu
from jax.sharding import PartitionSpec as P

ADAPTER_RANK = 16


adapter_scale = 2.0


MESH = pl.DeviceIdType.MESH
TILE_ROWS = 16
LANES = 128


def exchange_kernel(
    experts,
    blocks,
    facts,
    piece,
    maps,
    rows,
    facts_in,
    other_piece,
    maps_whole,
    row_send,
    row_recv,
    fact_send,
    fact_recv,
    pass_send,
    pass_recv,
    pair_send,
    pair_recv,
    own_sem,
):
    expert = lax.axis_index("expert")
    tensor = lax.axis_index("tensor")
    width = blocks.shape[2]
    columns = pl.ds(pl.multiple_of(tensor * width, LANES), width)
    partner = (expert, 1 - tensor)

    barrier = pltpu.get_barrier_semaphore()

    @pl.loop(1, experts)
    def _(step):
        peer = lax.rem(expert + step, experts)
        pl.semaphore_signal(barrier, inc=1, device_id=(peer, tensor), device_id_type=MESH)

    pl.semaphore_signal(barrier, inc=1, device_id=partner, device_id_type=MESH)
    pl.semaphore_wait(barrier, experts)

    def remote(source, target, send, recv, device):
        return pltpu.make_async_remote_copy(
            src_ref=source,
            dst_ref=target,
            send_sem=send,
            recv_sem=recv,
            device_id=device,
            device_id_type=MESH,
        )

    def row_copy(step):
        peer = lax.rem(expert + step, experts)
        return remote(
            blocks.at[peer],
            rows.at[expert, :, columns],
            row_send.at[step],
            row_recv.at[step],
            (peer, tensor),
        )

    def fact_copy(step):
        peer = lax.rem(expert + step, experts)
        return remote(
            facts.at[peer],
            facts_in.at[expert],
            fact_send.at[step],
            fact_recv.at[step],
            (peer, tensor),
        )

    def pass_copy(step):
        source = lax.rem(expert - step + experts, experts)
        return remote(
            rows.at[source, :, columns],
            rows.at[source, :, columns],
            pass_send.at[step],
            pass_recv.at[step],
            partner,
        )

    def far_first(index):
        return experts // 2 + (1 - 2 * (index % 2)) * ((index + 1) // 2)

    @pl.loop(0, experts - 1)
    def _(index):
        row_copy(far_first(index)).start()

    @pl.loop(1, experts)
    def _(step):
        fact_copy(step).start()

    own_copies = [
        pltpu.make_async_copy(blocks.at[expert], rows.at[expert, :, columns], own_sem.at[0]),
        pltpu.make_async_copy(facts.at[expert], facts_in.at[expert], own_sem.at[1]),
        pltpu.make_async_copy(maps, maps_whole.at[:, columns], own_sem.at[2]),
    ]
    pair_copies = [
        remote(piece, other_piece, pair_send.at[0], pair_recv.at[0], partner),
        remote(maps, maps_whole.at[:, columns], pair_send.at[1], pair_recv.at[1], partner),
        remote(
            blocks.at[expert],
            rows.at[expert, :, columns],
            pair_send.at[2],
            pair_recv.at[2],
            partner,
        ),
    ]
    for copy in own_copies + pair_copies:
        copy.start()

    @pl.loop(0, experts - 1)
    def _(index):
        row_copy(far_first(index)).wait_recv()
        pass_copy(far_first(index)).start()

    for copy in own_copies + pair_copies:
        copy.wait()

    @pl.loop(1, experts)
    def _(step):
        fact_copy(step).wait()
        row_copy(step).wait_send()
        pass_copy(step).wait()


def exchange(blocks, facts, piece, maps):
    experts, per_source, width = blocks.shape
    anywhere = pl.BlockSpec(memory_space=pl.ANY)
    sems = pltpu.SemaphoreType.DMA
    return pl.pallas_call(
        functools.partial(exchange_kernel, experts),
        out_shape=(
            jax.ShapeDtypeStruct((experts, per_source, 2 * width), blocks.dtype),
            jax.ShapeDtypeStruct(facts.shape, facts.dtype),
            jax.ShapeDtypeStruct(piece.shape, piece.dtype),
            jax.ShapeDtypeStruct((maps.shape[0], 2 * width), maps.dtype),
        ),
        in_specs=[anywhere] * 4,
        out_specs=(anywhere,) * 4,
        scratch_shapes=[sems((experts,))] * 6 + [sems((3,))] * 3,
        compiler_params=pltpu.CompilerParams(collective_id=0, has_side_effects=True),
        name="exchange",
    )(blocks, facts, piece, maps)


def fits_exchange(experts, per_source, width):
    return (
        lax.axis_size("tensor") == 2
        and per_source % TILE_ROWS == 0
        and 2 * per_source <= LANES
        and width % LANES == 0
        and experts % 2 == 0
    )


def silu_parts(gate):
    sig = jax.nn.sigmoid(gate)
    return (gate * sig, sig * (1.0 + gate * (1.0 - sig)))


def local(
    cotangent,
    routes,
    router_weight,
    clients,
    gate_preactivation,
    up_preactivation,
    down_matrix,
    adapter_input_maps,
    adapter_output_maps,
):
    experts = lax.axis_size("expert")
    tok_rows = cotangent.shape[0]
    width = cotangent.shape[1]
    picks_per = routes.shape[1]
    slots = gate_preactivation.shape[1]
    per_source = slots // experts
    adapter_groups = adapter_input_maps.shape[2] // ADAPTER_RANK
    token_ids = jnp.arange(tok_rows, dtype=jnp.int32)
    expert_ids = jnp.arange(experts, dtype=jnp.int32)
    slot_ids = jnp.arange(experts * per_source, dtype=jnp.int32)
    hits = (routes[:, :, None] == expert_ids).astype(jnp.float32)
    earlier = (token_ids[:, None] > token_ids[None, :]).astype(jnp.bfloat16)
    before = jnp.dot(
        earlier, jnp.sum(hits, axis=1).astype(jnp.bfloat16), preferred_element_type=jnp.float32
    )
    rank = jnp.sum(before[:, None, :] * hits, axis=2).astype(jnp.int32)
    slot = routes * per_source + rank
    chosen = [slot_ids[:, None] == slot[None, :, k] for k in range(picks_per)]
    filled = functools.reduce(jnp.logical_or, chosen)
    weight_slots = sum(
        jnp.sum(jnp.where(chosen[k], router_weight[None, :, k], 0.0), axis=1)
        for k in range(picks_per)
    )
    client_slots = jnp.sum(
        jnp.where(filled, (clients[None, :] + 1).astype(jnp.float32), 0.0), axis=1
    )
    facts = jnp.concatenate(
        [weight_slots.reshape(experts, per_source), client_slots.reshape(experts, per_source)],
        axis=1,
    )
    buffer = jnp.dot(
        filled.astype(jnp.bfloat16), cotangent, preferred_element_type=jnp.float32
    ).astype(cotangent.dtype)
    act, slope = silu_parts(gate_preactivation[0].astype(jnp.float32))
    up_full = up_preactivation[0].astype(jnp.float32)
    hidden_units = act * up_full
    hidden_lowrank = hidden_units.astype(jnp.bfloat16)
    contract_dims = (((1,), (1,)), ((), ()))
    row_dimensions = (((0,), (0,)), ((), ()))
    unmasked_piece = jnp.dot(
        hidden_lowrank, adapter_input_maps[0], preferred_element_type=jnp.float32
    )
    blocks = buffer.reshape(experts, per_source, width)
    if fits_exchange(experts, per_source, width):
        tiles = jnp.zeros((experts, 8, LANES), jnp.float32)
        tiles = lax.dynamic_update_slice(tiles, facts[:, None, :], (0, 0, 0))
        arrived, tiles_in, other_piece, output_map_whole = exchange(
            blocks, tiles, unmasked_piece, adapter_output_maps[0]
        )
        facts_in = tiles_in[:, 0, : 2 * per_source]
        token_rows = arrived.reshape(slots, 2 * width)
        part = lax.dynamic_slice_in_dim(token_rows, lax.axis_index("tensor") * width, width, 1)
        unmasked_rows = unmasked_piece + other_piece
    else:
        facts_in = lax.all_to_all(facts, "expert", split_axis=0, concat_axis=0, tiled=True)
        part = lax.all_to_all(
            blocks, "expert", split_axis=0, concat_axis=0, tiled=True
        ).reshape(slots, width)
        token_rows = lax.all_gather(part, "tensor", axis=1, tiled=True)
        output_map_whole = lax.all_gather(adapter_output_maps[0], "tensor", axis=1, tiled=True)
        unmasked_rows = lax.psum(unmasked_piece, "tensor")
    pick_weight = facts_in[:, :per_source].reshape(slots)
    column_client = jnp.arange(adapter_groups * ADAPTER_RANK, dtype=jnp.int32) // ADAPTER_RANK
    client_mask = (
        facts_in[:, per_source:].reshape(slots, 1) == (column_client + 1).astype(jnp.float32)
    ).astype(jnp.float32)
    frozen_output = lax.dot_general(
        token_rows, down_matrix[0], contract_dims, preferred_element_type=jnp.float32
    )
    projected_piece = unmasked_piece * client_mask
    projected_rows = unmasked_rows * client_mask
    local_terms = jnp.sum(hidden_units * frozen_output, axis=1)
    adapter_output = (
        lax.dot_general(
            token_rows, output_map_whole, contract_dims, preferred_element_type=jnp.float32
        )
        * client_mask
    )
    backward_result = lax.dot_general(
        adapter_output.astype(jnp.bfloat16),
        adapter_input_maps[0],
        contract_dims,
        preferred_element_type=jnp.float32,
    )
    hidden_gradient = pick_weight[:, None] * (frozen_output + adapter_scale * backward_result)
    gate_gradient = (hidden_gradient * up_full * slope).astype(jnp.bfloat16)
    up_gradient = (hidden_gradient * act).astype(jnp.bfloat16)
    input_map_gradient = adapter_scale * lax.dot_general(
        hidden_lowrank,
        (pick_weight[:, None] * adapter_output).astype(jnp.bfloat16),
        row_dimensions,
        preferred_element_type=jnp.float32,
    )
    output_map_gradient = adapter_scale * lax.dot_general(
        (pick_weight[:, None] * projected_rows).astype(jnp.bfloat16),
        part,
        row_dimensions,
        preferred_element_type=jnp.float32,
    )
    slot_piece = local_terms + adapter_scale * jnp.sum(projected_piece * adapter_output, axis=1)
    tensors = lax.axis_size("tensor")
    outgoing = jnp.broadcast_to(
        slot_piece.reshape(experts, 1, per_source), (experts, tensors, per_source)
    ).reshape(experts * tensors, per_source)
    returned = lax.all_to_all(
        outgoing, ("expert", "tensor"), split_axis=0, concat_axis=0, tiled=True
    )
    slot_gradient = jnp.sum(returned.reshape(experts, tensors, per_source), axis=1).reshape(-1)
    gate_grad = jnp.stack(
        [
            jnp.sum(jnp.where(chosen[k], slot_gradient[:, None], 0.0), axis=0)
            for k in range(picks_per)
        ],
        axis=1,
    )
    return (
        gate_grad,
        gate_gradient[None],
        up_gradient[None],
        input_map_gradient[None],
        output_map_gradient[None],
    )


def solution(mesh):
    in_specs = (
        P("expert", "tensor"),
        P("expert", None),
        P("expert", None),
        P("expert"),
        P("expert", None, "tensor"),
        P("expert", None, "tensor"),
        P("expert", "tensor", None),
        P("expert", "tensor", None),
        P("expert", None, "tensor"),
    )
    out_specs = (
        P("expert", None),
        P("expert", None, "tensor"),
        P("expert", None, "tensor"),
        P("expert", "tensor", None),
        P("expert", None, "tensor"),
    )
    return jax.shard_map(local, mesh=mesh, in_specs=in_specs, out_specs=out_specs, check_vma=False)
```
